128 devices in a mesh: seq: 16 (over z, y_lo, core), tp: 8 (over x, y_hi).
Axes of the slice: x: 4, y: 4 (y_hi: 2, y_lo: 2; y = y_hi * 2 + y_lo), z: 4, core: 2. Of those that a mesh axis runs over, the one named last changes fastest.
Arguments:
- layer_input: bfloat16 [16, 512, 4096], P('seq')
- memory: bfloat16 [16, 512, 4096], P('seq'), may hold values from -6 to 6
- seg_lengths: int32 [16], replicated, may hold values from 257 to 512, as said below
- query_weight: bfloat16 [4096, 4096], P(None, 'tp')
- key_weight: bfloat16 [4096, 4096], P(None, 'tp')
- value_weight: bfloat16 [4096, 4096], P(None, 'tp'), may hold values from -0.09375 to 0.09375
- out_weight: bfloat16 [4096, 4096], P('tp'), may hold values from -0.1875 to 0.1875
Outputs:
- attended: bfloat16 [16, 512, 4096], P('seq', 'tp')
The draws below stay inside these ranges and needn't reach their ends.
Inputs may be any that keep to these rules, and one draw needn't show every extreme that they name: `seg_lengths`: slots below a segment's count hold real tokens.
All inputs are finite; a program needn't handle non-finite values.
Results may differ from the reference program's by a relative error of at most 0.011.
Values may be sent and summed in bfloat16 or wider, within the bound.
A program may use at most 128 MiB of HBM per device.

```python
import math
import jax
import jax.numpy as jnp
from jax import lax

D = 4096
HEADS = 32
HEAD_DIM = 128
SEG = 512
SEGS_DEV = 1
NSEGS = 16
N_SEQ = 16


def attention_pair(key):
    base = jax.random.normal(jax.random.fold_in(key, 11), (D, D), jnp.float32)
    other = jax.random.normal(jax.random.fold_in(key, 12), (D, D), jnp.float32)
    return (base, other)


def draw_query_weight(key, part):
    base, other = attention_pair(key)
    return (base * (1.5 / math.sqrt(D))).astype(jnp.bfloat16)


def draw_key_weight(key, part):
    base, other = attention_pair(key)
    mixed = other
    return (mixed * (1.5 / math.sqrt(D))).astype(jnp.bfloat16)


def draw_layer_input(key, part):
    states = jax.random.truncated_normal(jax.random.fold_in(key, 21), -6.0, 6.0, (NSEGS, SEG, D), jnp.float32)
    return states.astype(jnp.bfloat16)


def draw_seg_lengths(key, part):
    short_by = jax.random.randint(jax.random.fold_in(key, 31), (NSEGS,), 0, SEG // 2)
    first_pick = jax.random.randint(jax.random.fold_in(key, 32), (), 0, NSEGS)
    second_pick = jnp.mod(first_pick + 1 + jax.random.randint(jax.random.fold_in(key, 33), (), 0, NSEGS - 1), NSEGS)
    short_by = short_by.at[first_pick].set(0)
    short_by = short_by.at[second_pick].set(SEG // 2 - 1)
    return (SEG - short_by).astype(jnp.int32)


def block_levels(stream_key, dims, shards, least, high):
    def one(axis_at, shards_of):
        heights = jax.random.uniform(jax.random.fold_in(jax.random.fold_in(stream_key, 6), axis_at), (shards_of,), jnp.float32, least / len(shards), high / len(shards))
        return jnp.repeat(jnp.exp(heights), dims[axis_at] // shards_of).reshape((-1,) + (1,) * (len(dims) - axis_at - 1))

    loudness = one(*shards[0])
    for cut in shards[1:]:
        loudness = loudness * one(*cut)
    return loudness


def centred(rng, shape, width, most, cuts=(), kind=jnp.bfloat16):
    result = width * jax.random.normal(rng, shape, jnp.float32)
    if cuts:
        result = result * block_levels(rng, shape, cuts, -0.22, 0.18)
    return jnp.clip(result, -most, most).astype(kind)


def setup_inputs(seed: int = 0) -> dict:
    key_of = jax.random.split(jax.random.key(seed), 8)
    return {
        "layer_input": draw_layer_input(jax.random.fold_in(key_of[7], 71), 0),
        "memory": centred(key_of[1], (N_SEQ, SEG, D), 1.0, 6.0, ((0, 16),)),
        "seg_lengths": draw_seg_lengths(jax.random.fold_in(key_of[7], 71), 0),
        "query_weight": draw_query_weight(jax.random.fold_in(key_of[7], 71), 0),
        "key_weight": draw_key_weight(jax.random.fold_in(key_of[7], 71), 0),
        "value_weight": centred(key_of[5], (D, D), D ** -0.5, 0.09375, ((1, 8),)),
        "out_weight": centred(key_of[6], (D, D), (D // 4) ** -0.5, 0.1875, ((0, 8),)),
    }


def attend_heads(queries, all_keys, all_values, key_ok):
    scores = jnp.einsum('qhd,khd->hqk', queries.astype(jnp.float32), all_keys.astype(jnp.float32)) / math.sqrt(HEAD_DIM)
    row_max = lax.optimization_barrier(jnp.max(jnp.where(key_ok[None], scores, -1e+30), axis=-1, keepdims=True))
    weights = jnp.where(key_ok[None], jnp.exp(scores - row_max), 0.0)
    probabilities = (weights / lax.optimization_barrier(jnp.sum(weights, axis=-1, keepdims=True))).astype(jnp.bfloat16)
    context = jnp.einsum('hqk,khd->qhd', probabilities.astype(jnp.float32), all_values.astype(jnp.float32))
    return context.astype(jnp.bfloat16)

def project(states, weight):
    return jnp.dot(states, weight, preferred_element_type=jnp.float32).astype(jnp.bfloat16)

def segment_step(inputs, mem_states, mem_len, own_len, query_weight, key_weight, value_weight, out_weight):
    seg_rows = inputs.shape[0]
    queries = project(inputs, query_weight).reshape(seg_rows, HEADS, HEAD_DIM)
    own_keys = project(inputs, key_weight).reshape(seg_rows, HEADS, HEAD_DIM)
    own_values = project(inputs, value_weight).reshape(seg_rows, HEADS, HEAD_DIM)
    mem_keys = project(mem_states, key_weight).reshape(seg_rows, HEADS, HEAD_DIM)
    mem_values = project(mem_states, value_weight).reshape(seg_rows, HEADS, HEAD_DIM)
    row_ids = jnp.arange(seg_rows, dtype=jnp.int32)[:, None]
    col_ids = jnp.arange(seg_rows, dtype=jnp.int32)[None, :]
    mem_ok = jnp.broadcast_to(col_ids < mem_len, (seg_rows, seg_rows))
    own_ok = (col_ids <= row_ids) & (col_ids < own_len)
    key_ok = jnp.concatenate([mem_ok, own_ok], axis=1)
    all_keys = jnp.concatenate([mem_keys, own_keys], axis=0)
    all_values = jnp.concatenate([mem_values, own_values], axis=0)
    context = attend_heads(queries, all_keys, all_values, key_ok).reshape(seg_rows, D)
    return jnp.dot(context, out_weight, preferred_element_type=jnp.float32).astype(jnp.bfloat16)

def reference(layer_input, memory, seg_lengths, query_weight, key_weight, value_weight, out_weight):

    def run_group(group_index):
        incoming = lax.dynamic_index_in_dim(memory, jnp.mod(group_index - 1, N_SEQ).astype(jnp.int32), 0, keepdims=False)
        mem_len = lax.dynamic_index_in_dim(seg_lengths, jnp.mod(group_index * SEGS_DEV - 1, NSEGS).astype(jnp.int32), 0, keepdims=False)
        results = []
        for seg_index in range(SEGS_DEV):
            position = (group_index * SEGS_DEV + seg_index).astype(jnp.int32)
            inputs = lax.dynamic_index_in_dim(layer_input, position, 0, keepdims=False)
            own_len = lax.dynamic_index_in_dim(seg_lengths, position, 0, keepdims=False)
            output = segment_step(inputs, incoming, mem_len, own_len, query_weight, key_weight, value_weight, out_weight)
            results.append(output)
            incoming = output
            mem_len = own_len
        return jnp.stack(results)
    grouped_out = lax.map(run_group, jnp.arange(N_SEQ, dtype=jnp.int32))
    return grouped_out.reshape(NSEGS, SEG, D)
```

```python
import functools
import math

import jax
import jax.numpy as jnp
from jax import lax
from jax.experimental import pallas as pl
from jax.experimental.pallas import tpu as pltpu
from jax.sharding import PartitionSpec as P

F32 = jnp.float32
BF16 = jnp.bfloat16
MESH = pl.DeviceIdType.MESH

SEG = 512
D = 4096
HD = 128
COLS = 512
PAIR = 256
TW = 512
NT = D // TW
Q_SCALE = math.log2(math.e) / math.sqrt(HD)
MASKED = -3e38
D_ORDER = (2, 1, 3, 0)


def kernel(
    lens,
    x_hbm,
    mem_hbm,
    wq_hbm,
    wk_hbm,
    wv_hbm,
    wo_hbm,
    out_ref,
    x_v,
    mem_v,
    w_v,
    wo_v,
    wof,
    kv_send,
    kv_recv,
    own,
    ctx_send,
    ctx_recv,
    ctx_own,
    p_buf,
    r1,
    rb,
    rf,
    ld_sem,
    kvs,
    kvr,
    cxs,
    cxr,
    wcs,
    wcr,
    wzs,
    wzr,
    wbs,
    wbr,
    r1s,
    r1r,
    rbs,
    rbr,
    rfs,
    rfr,
):
    s = lax.axis_index("seq")
    t = lax.axis_index("tp")
    core = lax.rem(s, 2)
    yl = lax.rem(s // 2, 2)
    z = s // 4
    x = t // 2
    yh = lax.rem(t, 2)

    def at(seq, tp):
        return {"seq": seq, "tp": tp}

    following = at(lax.rem(s + 1, 16), t)
    previous = at(lax.rem(s + 15, 16), t)
    partner = at(s, x * 2 + 1 - yh)
    cross = at(z * 4 + (1 - yl) * 2 + core, x * 2 + 1 - yh)
    sibling = at(s + 1 - 2 * core, t)

    def along_z(by):
        return at(lax.rem(z + by + 4, 4) * 4 + yl * 2 + core, t)

    def along_x(by):
        return at(s, lax.rem(x + by + 4, 4) * 2 + yh)

    barrier = pltpu.get_barrier_semaphore()
    for peer in (
        following,
        previous,
        partner,
        cross,
        along_z(1),
        along_z(-1),
        along_x(1),
        along_x(-1),
    ):
        pl.semaphore_signal(barrier, inc=1, device_id=peer, device_id_type=MESH)

    def load_w(src, pair, kind):
        c = pair * 3 + kind
        return pltpu.make_async_copy(
            src.at[:, pl.ds(pair * PAIR, PAIR)], w_v.at[c], ld_sem.at[c]
        )

    load_mem = pltpu.make_async_copy(mem_hbm.at[0], mem_v, ld_sem.at[6])
    load_x = pltpu.make_async_copy(x_hbm.at[0], x_v, ld_sem.at[7])
    load_wo = pltpu.make_async_copy(wo_hbm, wo_v, ld_sem.at[8])
    load_mem.start()
    load_w(wk_hbm, 0, 0).start()
    load_w(wv_hbm, 0, 1).start()
    load_w(wk_hbm, 1, 0).start()
    load_w(wv_hbm, 1, 1).start()
    load_x.start()
    load_w(wq_hbm, 0, 2).start()
    load_w(wq_hbm, 1, 2).start()
    load_wo.start()

    def remote(src, dst, send, recv, to):
        return pltpu.make_async_remote_copy(
            src_ref=src,
            dst_ref=dst,
            send_sem=send,
            recv_sem=recv,
            device_id=to,
            device_id_type=MESH,
        )

    def wait_w(c):
        pltpu.make_async_copy(w_v.at[c], w_v.at[c], ld_sem.at[c]).wait()

    def kv_copy(c):
        return remote(kv_send.at[c], kv_recv.at[c], kvs.at[c], kvr.at[c], following)

    def tile(zz, cc):
        return lax.rem(zz + 4, 4) * 2 + cc

    half = COLS // 2

    def cross_copy(i):
        if i < 2:
            g = tile(z, core)
            rows = pl.ds(i * half, half)
        else:
            g = tile(z + 2, core)
            rows = pl.ds(0, COLS)
        return remote(
            wo_hbm.at[rows, pl.ds(pl.multiple_of(g * TW, TW), TW)],
            wof.at[g, rows],
            wcs.at[i],
            wcr.at[i],
            cross,
        )

    def z_copy(by, i, zz):
        g = tile(zz, core)
        rows = pl.ds(i * half, half)
        k = (1 - by) + i
        return remote(
            wof.at[g, rows], wof.at[g, rows], wzs.at[k], wzr.at[k], along_z(by)
        )

    def sibling_copy(i, cc):
        g = tile(z + (0, 1, -1, 2)[i], cc)
        return remote(wof.at[g], wof.at[g], wbs.at[i], wbr.at[i], sibling)

    load_mem.wait()

    def mem_step(c, _):
        w = c + c // 2
        wait_w(w)
        kv_send[c] = jnp.dot(mem_v[...], w_v[w], preferred_element_type=F32).astype(BF16)

        @pl.when(c == 0)
        def _():
            pl.semaphore_wait(barrier, 8)
            for i in range(3):
                cross_copy(i).start()

        kv_copy(c).start()
        return 0

    lax.fori_loop(0, 4, mem_step, 0)
    load_x.wait()

    own_len = lens[s]
    mem_len = lens[lax.rem(s + 15, 16)]

    def row_start(d, which):
        return (lax.rem(x + d, 4) * 2 + which) * 64

    def attend(pair, which, dst):
        rows = [pl.ds(pl.multiple_of(row_start(d, which), 64), 64) for d in D_ORDER]
        ids = jnp.concatenate(
            [
                lax.broadcasted_iota(jnp.int32, (64, 1), 0) + row_start(d, which)
                for d in D_ORDER
            ],
            axis=0,
        )
        last = jnp.minimum(ids, own_len - 1)
        col = lax.broadcasted_iota(jnp.int32, (1, SEG), 1)
        ones = jnp.ones((SEG, HD), BF16)
        for hh in range(2):
            cs = slice(hh * HD, (hh + 1) * HD)
            q = jnp.concatenate([own[pair * 3 + 2, r, cs] for r in rows], axis=0)
            dims = (((1,), (1,)), ((), ()))
            s_mem = lax.dot_general(
                q, kv_recv[pair * 2, :, cs], dims, preferred_element_type=F32
            )
            s_own = lax.dot_general(
                q, own[pair * 3, :, cs], dims, preferred_element_type=F32
            )
            s_mem = jnp.where(col < mem_len, s_mem, MASKED)
            s_own = jnp.where(col <= last, s_own, MASKED)
            top = jnp.max(jnp.maximum(s_mem, s_own), axis=1, keepdims=True)
            w_mem = jnp.exp2(s_mem - top).astype(BF16)
            w_own = jnp.exp2(s_own - top).astype(BF16)
            v_mem = jnp.concatenate([kv_recv[pair * 2 + 1, :, cs], ones], axis=1)
            v_own = jnp.concatenate([own[pair * 3 + 1, :, cs], ones], axis=1)
            r = jnp.dot(w_mem, v_mem, preferred_element_type=F32) + jnp.dot(
                w_own, v_own, preferred_element_type=F32
            )
            dst[pair, :, cs] = (r[:, :HD] / r[:, HD:]).astype(BF16)

    def ctx_copy(pair, i):
        rows = pl.ds(i * 128, 128)
        k = pair * 2 + i
        return remote(
            ctx_send.at[pair, rows], ctx_recv.at[pair, rows], cxs.at[k], cxr.at[k], partner
        )

    def own_step(c, _):
        pair = c // 3

        @pl.when(lax.rem(c, 3) == 2)
        def _():
            wait_w(c)

        scale = jnp.where(lax.rem(c, 3) == 2, Q_SCALE, 1.0).astype(F32)
        own[c] = (
            jnp.dot(x_v[...], w_v[c], preferred_element_type=F32) * scale
        ).astype(BF16)

        @pl.when(c == 2)
        def _():
            cross_copy(0).wait_recv()
            z_copy(1, 0, z).start()
            z_copy(-1, 0, z).start()

        @pl.when(c == 4)
        def _():
            cross_copy(1).wait_recv()
            z_copy(1, 1, z).start()
            z_copy(-1, 1, z).start()
            sibling_copy(0, core).start()

        @pl.when(lax.rem(c, 3) == 2)
        def _():
            kv_copy(pair * 2).wait_recv()
            kv_copy(pair * 2 + 1).wait_recv()
            attend(pair, 1 - yh, ctx_send)
            ctx_copy(pair, 0).start()
            ctx_copy(pair, 1).start()
            attend(pair, yh, ctx_own)

        return 0

    lax.fori_loop(0, 6, own_step, 0)
    load_wo.wait()
    for pair in range(2):
        for i in range(2):
            ctx_copy(pair, i).wait_recv()

    def tile_of(k):
        j = k // 2
        off = j + j // 2 - 2 * (j // 3)
        par = lax.rem(k, 2)
        return tile(z + off, core + par * (1 - 2 * core))

    def far_copy(k):
        sgn = 1 - 2 * lax.rem(k, 2)
        return remote(
            p_buf.at[k, pl.ds(0, 64)], r1.at[k], r1s.at[k], r1r.at[k], along_x(sgn)
        )

    def back_copy(k):
        par = lax.rem(k, 2)
        rows = pl.ds(pl.multiple_of(128 - 64 * par, 64), 64)
        return remote(
            p_buf.at[k, rows], rb.at[k], rbs.at[k], rbr.at[k], along_x(2 * par - 1)
        )

    def fwd_rows(k):
        return pl.ds(pl.multiple_of(64 + 64 * lax.rem(k, 2), 64), 64)

    def fwd_copy(k):
        return remote(
            p_buf.at[k, fwd_rows(k)],
            rf.at[k],
            rfs.at[k],
            rfr.at[k],
            along_x(1 - 2 * lax.rem(k, 2)),
        )

    def project_tile(k):
        g = tile_of(k)
        cols = pl.ds(pl.multiple_of(g * TW, TW), TW)
        acc = jnp.dot(ctx_own[0], wo_v[0:PAIR, cols], preferred_element_type=F32)
        acc += jnp.dot(ctx_own[1], wo_v[PAIR:COLS, cols], preferred_element_type=F32)
        acc += jnp.dot(ctx_recv[0], wof[g, 0:PAIR], preferred_element_type=F32)
        acc += jnp.dot(ctx_recv[1], wof[g, PAIR:COLS], preferred_element_type=F32)
        p_buf[k] = acc.astype(BF16)
        far_copy(k).start()
        back_copy(k).start()

    def combine(k):
        far_copy(k).wait_recv()
        rows = fwd_rows(k)
        p_buf[k, rows] = (p_buf[k, rows].astype(F32) + r1[k].astype(F32)).astype(BF16)
        fwd_copy(k).start()

    def finish(k):
        back_copy(k).wait_recv()
        fwd_copy(k).wait_recv()
        g = tile_of(k)
        cols = pl.ds(pl.multiple_of(g * TW, TW), TW)
        out_ref[:, cols] = (
            p_buf[k, 192:256].astype(F32) + rb[k].astype(F32) + rf[k].astype(F32)
        ).astype(BF16)

    def out_step(k, _):
        for j in range(4):

            @pl.when(k == 2 * j)
            def _(j=j):
                if j == 1:
                    z_copy(-1, 0, z + 1).wait_recv()
                    z_copy(-1, 1, z + 1).wait_recv()
                if j == 2:
                    z_copy(1, 0, z - 1).wait_recv()
                    z_copy(1, 1, z - 1).wait_recv()
                if j == 3:
                    cross_copy(2).wait_recv()
                if j > 0:
                    sibling_copy(j, core).start()

            @pl.when(k == 2 * j + 1)
            def _(j=j):
                sibling_copy(j, 1 - core).wait_recv()

        @pl.when(k < NT)
        def _():
            project_tile(k)

        @pl.when(k >= 2)
        def _():
            combine(k - 2)

        return 0

    lax.fori_loop(0, NT + 2, out_step, 0)

    def last_step(k, _):
        finish(k)
        return 0

    lax.fori_loop(0, NT, last_step, 0)

    for c in range(4):
        kv_copy(c).wait_send()
        sibling_copy(c, core).wait_send()
        ctx_copy(c // 2, c % 2).wait_send()
    for i in range(3):
        cross_copy(i).wait_send()
    for i in range(2):
        z_copy(1, i, z).wait_send()
        z_copy(-1, i, z).wait_send()

    def drain(k, _):
        far_copy(k).wait_send()
        back_copy(k).wait_send()
        fwd_copy(k).wait_send()
        return 0

    lax.fori_loop(0, NT, drain, 0)


def body(layer_input, memory, seg_lengths, query_weight, key_weight, value_weight, out_weight):
    dma = pltpu.SemaphoreType.DMA
    out = pl.pallas_call(
        kernel,
        out_shape=jax.ShapeDtypeStruct((64, D), BF16),
        in_specs=[pl.BlockSpec(memory_space=pltpu.SMEM)]
        + [pl.BlockSpec(memory_space=pl.ANY)] * 6,
        out_specs=pl.BlockSpec(memory_space=pltpu.VMEM),
        scratch_shapes=[
            pltpu.VMEM((SEG, D), BF16),
            pltpu.VMEM((SEG, D), BF16),
            pltpu.VMEM((6, D, PAIR), BF16),
            pltpu.VMEM((COLS, D), BF16),
            pltpu.VMEM((NT, COLS, TW), BF16),
            pltpu.VMEM((4, SEG, PAIR), BF16),
            pltpu.VMEM((4, SEG, PAIR), BF16),
            pltpu.VMEM((6, SEG, PAIR), BF16),
            pltpu.VMEM((2, 256, PAIR), BF16),
            pltpu.VMEM((2, 256, PAIR), BF16),
            pltpu.VMEM((2, 256, PAIR), BF16),
            pltpu.VMEM((NT, 256, TW), BF16),
            pltpu.VMEM((NT, 64, TW), BF16),
            pltpu.VMEM((NT, 64, TW), BF16),
            pltpu.VMEM((NT, 64, TW), BF16),
            dma((9,)),
            dma((4,)),
            dma((4,)),
            dma((4,)),
            dma((4,)),
            dma((3,)),
            dma((3,)),
            dma((4,)),
            dma((4,)),
            dma((4,)),
            dma((4,)),
            dma((NT,)),
            dma((NT,)),
            dma((NT,)),
            dma((NT,)),
            dma((NT,)),
            dma((NT,)),
        ],
        compiler_params=pltpu.CompilerParams(
            collective_id=0, has_side_effects=True, vmem_limit_bytes=60 * 2**20
        ),
    )(
        seg_lengths,
        layer_input,
        memory,
        query_weight,
        key_weight,
        value_weight,
        out_weight,
    )
    return out[None]


def solution(mesh):
    return jax.shard_map(
        body,
        mesh=mesh,
        in_specs=(
            P("seq", None, None),
            P("seq", None, None),
            P(),
            P(None, "tp"),
            P(None, "tp"),
            P(None, "tp"),
            P("tp", None),
        ),
        out_specs=P("seq", "tp", None),
        check_vma=False,
    )
```

```python
import functools
import math

import jax
import jax.numpy as jnp
from jax import lax
from jax.experimental import pallas as pl
from jax.experimental.pallas import tpu as pltpu
from jax.sharding import PartitionSpec as P

F32 = jnp.float32
BF16 = jnp.bfloat16
MESH = pl.DeviceIdType.MESH

SEG = 512
D = 4096
HD = 128
COLS = 512
PAIR = 256
PART = 1024
TW = 512
NT = D // TW
SCALE = math.log2(math.e) / math.sqrt(HD)
MASKED = -3e38
D_ORDER = (2, 1, 3, 0)


def kernel(
    lens,
    x_hbm,
    mem_hbm,
    wq_hbm,
    wk_hbm,
    wv_hbm,
    wo_hbm,
    out_ref,
    states,
    w_v,
    wo_v,
    wof,
    kv_send,
    kv_recv,
    made,
    ctx,
    ctx_recv,
    first,
    p_loc,
    p_buf,
    r1,
    rb,
    rf,
    ld_sem,
    kvs,
    kvr,
    cxs,
    cxr,
    wcs,
    wcr,
    wzs,
    wzr,
    wbs,
    wbr,
    r1s,
    r1r,
    rbs,
    rbr,
    rfs,
    rfr,
):
    s = lax.axis_index("seq")
    t = lax.axis_index("tp")
    core = lax.rem(s, 2)
    yl = lax.rem(s // 2, 2)
    z = s // 4
    x = t // 2
    yh = lax.rem(t, 2)

    def at(seq, tp):
        return {"seq": seq, "tp": tp}

    following = at(lax.rem(s + 1, 16), t)
    previous = at(lax.rem(s + 15, 16), t)
    partner = at(s, x * 2 + 1 - yh)
    cross = at(z * 4 + (1 - yl) * 2 + core, x * 2 + 1 - yh)
    sibling = at(s + 1 - 2 * core, t)

    def along_z(by):
        return at(lax.rem(z + by + 4, 4) * 4 + yl * 2 + core, t)

    def along_x(by):
        return at(s, lax.rem(x + by + 4, 4) * 2 + yh)

    barrier = pltpu.get_barrier_semaphore()
    for peer in (
        following,
        previous,
        partner,
        cross,
        along_z(1),
        along_z(-1),
        along_x(1),
        along_x(-1),
    ):
        pl.semaphore_signal(barrier, inc=1, device_id=peer, device_id_type=MESH)

    def load_w(src, pair, kind, part, depth, sem):
        rows = pl.ds(part * depth, depth)
        return pltpu.make_async_copy(
            src.at[rows, pl.ds(pair * PAIR, PAIR)],
            w_v.at[pair, rows, pl.ds(kind * PAIR, PAIR)],
            ld_sem.at[sem],
        )

    def first_loads(i):
        part = pl.ds(pl.multiple_of(i * PART, PART), PART)
        return (
            pltpu.make_async_copy(
                mem_hbm.at[0, :, part], states.at[0, :, part], ld_sem.at[i]
            ),
            load_w(wk_hbm, 0, 0, i, PART, 4 + i),
        )

    load_v0 = load_w(wv_hbm, 0, 1, 0, D, 8)

    load_kv1 = (
        load_w(wk_hbm, 1, 0, 0, D, 12),
        load_w(wv_hbm, 1, 1, 0, D, 13),
    )
    load_x = pltpu.make_async_copy(x_hbm.at[0], states.at[1], ld_sem.at[14])
    load_q = pltpu.make_async_copy(wq_hbm, w_v.at[2], ld_sem.at[15])
    load_wo = pltpu.make_async_copy(wo_hbm, wo_v, ld_sem.at[16])
    for i in range(2):
        for copy in first_loads(i):
            copy.start()

    def remote(src, dst, send, recv, to):
        return pltpu.make_async_remote_copy(
            src_ref=src,
            dst_ref=dst,
            send_sem=send,
            recv_sem=recv,
            device_id=to,
            device_id_type=MESH,
        )

    def kv_copy(c):
        return remote(kv_send.at[c], kv_recv.at[c], kvs.at[c], kvr.at[c], following)

    def tile(zz, cc):
        return lax.rem(zz + 4, 4) * 2 + cc

    half = COLS // 2

    def cross_copy(i):
        g = tile(z + 2 * (i // 2), core)
        rows = pl.ds((i % 2) * half, half)
        return remote(
            wo_hbm.at[rows, pl.ds(pl.multiple_of(g * TW, TW), TW)],
            wof.at[g, rows],
            wcs.at[i],
            wcr.at[i],
            cross,
        )

    def z_copy(by, i, zz):
        g = tile(zz, core)
        rows = pl.ds(i * half, half)
        k = (1 - by) + i
        return remote(
            wof.at[g, rows], wof.at[g, rows], wzs.at[k], wzr.at[k], along_z(by)
        )

    def sibling_copy(i, cc):
        g = tile(z + (0, 1, -1, 2)[i], cc)
        return remote(wof.at[g], wof.at[g], wbs.at[i], wbr.at[i], sibling)

    own_len = lens[s]
    mem_len = lens[lax.rem(s + 15, 16)]

    def row_start(d, which):
        return (lax.rem(x + d, 4) * 2 + which) * 64

    def at_column(c):
        return c if isinstance(c, int) else pl.multiple_of(c, HD)

    def attend(pairs, group):
        which = 1 - yh + group * (2 * yh - 1)
        starts = [row_start(d, which) for d in D_ORDER]
        rows = [pl.ds(pl.multiple_of(start, 64), 64) for start in starts]
        ids = jnp.concatenate(
            [lax.broadcasted_iota(jnp.int32, (64, 1), 0) + start for start in starts],
            axis=0,
        )
        last = jnp.minimum(ids, own_len - 1)
        col = lax.broadcasted_iota(jnp.int32, (1, SEG), 1)
        ones = jnp.ones((SEG, HD), BF16)
        for pair, hh in [(pair, hh) for pair in pairs for hh in range(2)]:
            ks = slice(hh * HD, (hh + 1) * HD)
            vs = slice(PAIR + hh * HD, PAIR + (hh + 1) * HD)
            qs = pl.ds(at_column(pair * PAIR + hh * HD), HD)
            q = jnp.concatenate([made[2, r, qs] for r in rows], axis=0)
            dims = (((1,), (1,)), ((), ()))
            s_mem = SCALE * lax.dot_general(
                q, kv_recv[2 * pair, :, ks], dims, preferred_element_type=F32
            )
            s_own = SCALE * lax.dot_general(
                q, made[3 + pair, :, ks], dims, preferred_element_type=F32
            )
            s_mem = jnp.concatenate(
                [
                    s_mem[:, :256],
                    jnp.where(col[:, 256:] < mem_len, s_mem[:, 256:], MASKED),
                ],
                axis=1,
            )
            s_own = jnp.where(col <= last, s_own, MASKED)
            top = jnp.max(jnp.maximum(s_mem, s_own), axis=1, keepdims=True)
            w_mem = jnp.exp2(s_mem - top).astype(BF16)
            w_own = jnp.exp2(s_own - top).astype(BF16)
            v_mem = jnp.concatenate([kv_recv[2 * pair + 1, :, ks], ones], axis=1)
            v_own = jnp.concatenate([made[3 + pair, :, vs], ones], axis=1)
            r = jnp.dot(w_mem, v_mem, preferred_element_type=F32) + jnp.dot(
                w_own, v_own, preferred_element_type=F32
            )
            ctx[group * 2 + pair, :, ks] = (r[:, :HD] / r[:, HD:]).astype(BF16)

    def ctx_copy(pair):
        return remote(
            ctx.at[pair], ctx_recv.at[pair], cxs.at[pair], cxr.at[pair], partner
        )

    def first_part(i, _):
        c = i // 4
        n = lax.rem(i, 4)

        @pl.when(i < 4)
        def _():
            for copy in first_loads(n):
                copy.wait()

        @pl.when(i < 2)
        def _():
            for copy in first_loads(n + 2):
                copy.start()

        @pl.when(i == 2)
        def _():
            load_v0.start()

        @pl.when(i == 4)
        def _():
            load_v0.wait()
            load_kv1[0].start()
            load_kv1[1].start()

        part = pl.ds(pl.multiple_of(n * PART, PART), PART)
        cols = pl.ds(pl.multiple_of(c * PAIR, PAIR), PAIR)
        term = jnp.dot(
            states[0, :, part], w_v[0, part, cols], preferred_element_type=F32
        )

        @pl.when(n == 0)
        def _():
            first[...] = term

        @pl.when(n > 0)
        def _():
            first[...] += term

        @pl.when(n == 3)
        def _():
            kv_send[c] = first[...].astype(BF16)

        @pl.when(i == 3)
        def _():
            pl.semaphore_wait(barrier, 8)

        @pl.when(n == 3)
        def _():
            kv_copy(c).start()

        @pl.when(i == 3)
        def _():
            cross_copy(0).start()
            cross_copy(1).start()

        return 0

    lax.fori_loop(0, 8, first_part, 0)

    def make(i, _):
        own_part = jnp.minimum(i // 2, 1)
        w = lax.rem(i, 3)

        @pl.when(i == 1)
        def _():
            load_x.start()
            load_q.start()
            load_kv1[0].wait()
            load_kv1[1].wait()

        @pl.when(i == 2)
        def _():
            load_x.wait()
            load_q.wait()
            load_wo.start()

        made[i] = jnp.dot(
            states[own_part], w_v[w], preferred_element_type=F32
        ).astype(BF16)

        @pl.when(i == 1)
        def _():
            for c in range(2):
                kv_send[2 + c] = made[1, :, c * PAIR : (c + 1) * PAIR]
                kv_copy(2 + c).start()

        @pl.when(i == 3)
        def _():
            cross_copy(0).wait_recv()
            z_copy(1, 0, z).start()
            z_copy(-1, 0, z).start()

        @pl.when(i == 4)
        def _():
            cross_copy(1).wait_recv()
            z_copy(1, 1, z).start()
            z_copy(-1, 1, z).start()
            sibling_copy(0, core).start()
            cross_copy(2).start()

        return 0

    def phase(ph, _):
        lax.fori_loop(1 + 3 * ph, 4 + ph, make, 0)
        kv_copy(2 * ph).wait_recv()
        kv_copy(2 * ph + 1).wait_recv()
        attend((ph,), 0)
        ctx_copy(ph).start()
        return 0

    lax.fori_loop(0, 2, phase, 0)
    cross_copy(3).start()
    attend((0, 1), 1)
    load_wo.wait()

    def both_pairs(ref, at_pair):
        return jnp.concatenate([ref[at_pair], ref[at_pair + 1]], axis=1)

    def local_step(i, _):
        cols = pl.ds(pl.multiple_of(i * 1024, 1024), 1024)
        p_loc[:, cols] = jnp.dot(
            both_pairs(ctx, 2), wo_v[:, cols], preferred_element_type=F32
        )
        return 0

    lax.fori_loop(0, 4, local_step, 0)
    ctx_copy(0).wait_recv()
    ctx_copy(1).wait_recv()

    def tile_of(k):
        j = k // 2
        off = j + j // 2 - 2 * (j // 3)
        par = lax.rem(k, 2)
        return tile(z + off, core + par * (1 - 2 * core))

    def far_copy(k):
        sgn = 1 - 2 * lax.rem(k, 2)
        return remote(
            p_buf.at[k, pl.ds(0, 64)], r1.at[k], r1s.at[k], r1r.at[k], along_x(sgn)
        )

    def back_copy(k):
        par = lax.rem(k, 2)
        rows = pl.ds(pl.multiple_of(128 - 64 * par, 64), 64)
        return remote(
            p_buf.at[k, rows], rb.at[k], rbs.at[k], rbr.at[k], along_x(2 * par - 1)
        )

    def fwd_rows(k):
        return pl.ds(pl.multiple_of(64 + 64 * lax.rem(k, 2), 64), 64)

    def fwd_copy(k):
        return remote(
            p_buf.at[k, fwd_rows(k)],
            rf.at[k],
            rfs.at[k],
            rfr.at[k],
            along_x(1 - 2 * lax.rem(k, 2)),
        )

    def project_tile(k):
        g = tile_of(k)
        cols = pl.ds(pl.multiple_of(g * TW, TW), TW)
        acc = p_loc[:, cols] + jnp.dot(
            both_pairs(ctx_recv, 0), wof[g], preferred_element_type=F32
        )
        p_buf[k] = acc.astype(BF16)
        far_copy(k).start()
        back_copy(k).start()

    def combine(k):
        far_copy(k).wait_recv()
        rows = fwd_rows(k)
        p_buf[k, rows] = (p_buf[k, rows].astype(F32) + r1[k].astype(F32)).astype(BF16)
        fwd_copy(k).start()

    def finish(k):
        back_copy(k).wait_recv()
        fwd_copy(k).wait_recv()
        g = tile_of(k)
        cols = pl.ds(pl.multiple_of(g * TW, TW), TW)
        out_ref[:, cols] = (
            p_buf[k, 192:256].astype(F32) + rb[k].astype(F32) + rf[k].astype(F32)
        ).astype(BF16)

    def out_step(k, _):
        for j in range(4):

            @pl.when(k == 2 * j)
            def _(j=j):
                if j == 1:
                    z_copy(-1, 0, z + 1).wait_recv()
                    z_copy(-1, 1, z + 1).wait_recv()
                if j == 2:
                    z_copy(1, 0, z - 1).wait_recv()
                    z_copy(1, 1, z - 1).wait_recv()
                if j == 3:
                    cross_copy(2).wait_recv()
                    cross_copy(3).wait_recv()
                if j > 0:
                    sibling_copy(j, core).start()

            @pl.when(k == 2 * j + 1)
            def _(j=j):
                sibling_copy(j, 1 - core).wait_recv()

        @pl.when(k < NT)
        def _():
            project_tile(k)

        @pl.when(k >= 4)
        def _():
            combine(k - 4)

        return 0

    lax.fori_loop(0, NT + 4, out_step, 0)

    def last_step(k, _):
        finish(k)
        return 0

    lax.fori_loop(0, NT, last_step, 0)

    for c in range(4):
        sibling_copy(c, core).wait_send()
        cross_copy(c).wait_send()
        kv_copy(c).wait_send()
    for pair in range(2):
        ctx_copy(pair).wait_send()
    for i in range(2):
        z_copy(1, i, z).wait_send()
        z_copy(-1, i, z).wait_send()

    def drain(k, _):
        far_copy(k).wait_send()
        back_copy(k).wait_send()
        fwd_copy(k).wait_send()
        return 0

    lax.fori_loop(0, NT, drain, 0)


def body(layer_input, memory, seg_lengths, query_weight, key_weight, value_weight, out_weight):
    dma = pltpu.SemaphoreType.DMA
    out = pl.pallas_call(
        kernel,
        out_shape=jax.ShapeDtypeStruct((64, D), BF16),
        in_specs=[pl.BlockSpec(memory_space=pltpu.SMEM)]
        + [pl.BlockSpec(memory_space=pl.ANY)] * 6,
        out_specs=pl.BlockSpec(memory_space=pltpu.VMEM),
        scratch_shapes=[
            pltpu.VMEM((2, SEG, D), BF16),
            pltpu.VMEM((3, D, COLS), BF16),
            pltpu.VMEM((COLS, D), BF16),
            pltpu.VMEM((NT, COLS, TW), BF16),
            pltpu.VMEM((4, SEG, PAIR), BF16),
            pltpu.VMEM((4, SEG, PAIR), BF16),
            pltpu.VMEM((5, SEG, COLS), BF16),
            pltpu.VMEM((4, 256, PAIR), BF16),
            pltpu.VMEM((2, 256, PAIR), BF16),
            pltpu.VMEM((SEG, PAIR), F32),
            pltpu.VMEM((256, D), F32),
            pltpu.VMEM((NT, 256, TW), BF16),
            pltpu.VMEM((NT, 64, TW), BF16),
            pltpu.VMEM((NT, 64, TW), BF16),
            pltpu.VMEM((NT, 64, TW), BF16),
            dma((17,)),
            dma((4,)),
            dma((4,)),
            dma((2,)),
            dma((2,)),
            dma((4,)),
            dma((4,)),
            dma((4,)),
            dma((4,)),
            dma((4,)),
            dma((4,)),
            dma((NT,)),
            dma((NT,)),
            dma((NT,)),
            dma((NT,)),
            dma((NT,)),
            dma((NT,)),
        ],
        compiler_params=pltpu.CompilerParams(
            collective_id=0, has_side_effects=True, vmem_limit_bytes=60 * 2**20
        ),
    )(
        seg_lengths,
        layer_input,
        memory,
        query_weight,
        key_weight,
        value_weight,
        out_weight,
    )
    return out[None]


def solution(mesh):
    return jax.shard_map(
        body,
        mesh=mesh,
        in_specs=(
            P("seq", None, None),
            P("seq", None, None),
            P(),
            P(None, "tp"),
            P(None, "tp"),
            P(None, "tp"),
            P("tp", None),
        ),
        out_specs=P("seq", "tp", None),
        check_vma=False,
    )
```

```python
import functools
import math

import jax
import jax.numpy as jnp
from jax import lax
from jax.experimental import pallas as pl
from jax.experimental.pallas import tpu as pltpu
from jax.sharding import PartitionSpec as P

F32 = jnp.float32
BF16 = jnp.bfloat16
MESH = pl.DeviceIdType.MESH

SEG = 512
D = 4096
HD = 128
COLS = 512
PAIR = 256
PART = 1024
TW = 512
NT = D // TW
SCALE = math.log2(math.e) / math.sqrt(HD)
MASKED = -3e38
D_ORDER = (2, 1, 3, 0)


def kernel(
    lens_hbm,
    x_hbm,
    mem_hbm,
    wq_hbm,
    wk_hbm,
    wv_hbm,
    wo_hbm,
    out_ref,
    lens,
    states,
    w_v,
    wo_v,
    wof,
    kv_send,
    kv_recv,
    made,
    ctx,
    ctx_recv,
    first,
    p_loc,
    p_buf,
    r1,
    rb,
    rf,
    ld_sem,
    kvs,
    kvr,
    cxs,
    cxr,
    wcs,
    wcr,
    wzs,
    wzr,
    wbs,
    wbr,
    r1s,
    r1r,
    rbs,
    rbr,
    rfs,
    rfr,
):
    s = lax.axis_index("seq")
    t = lax.axis_index("tp")
    core = lax.rem(s, 2)
    yl = lax.rem(s // 2, 2)
    z = s // 4
    x = t // 2
    yh = lax.rem(t, 2)

    def at(seq, tp):
        return {"seq": seq, "tp": tp}

    following = at(lax.rem(s + 1, 16), t)
    previous = at(lax.rem(s + 15, 16), t)
    partner = at(s, x * 2 + 1 - yh)
    cross = at(z * 4 + (1 - yl) * 2 + core, x * 2 + 1 - yh)
    sibling = at(s + 1 - 2 * core, t)

    def along_z(by):
        return at(lax.rem(z + by + 4, 4) * 4 + yl * 2 + core, t)

    def along_x(by):
        return at(s, lax.rem(x + by + 4, 4) * 2 + yh)

    barrier = pltpu.get_barrier_semaphore()
    for peer in (
        following,
        previous,
        partner,
        cross,
        along_z(1),
        along_z(-1),
        along_x(1),
        along_x(-1),
    ):
        pl.semaphore_signal(barrier, inc=1, device_id=peer, device_id_type=MESH)

    def load_w(src, pair, kind, part, depth, sem):
        rows = pl.ds(part * depth, depth)
        return pltpu.make_async_copy(
            src.at[rows, pl.ds(pair * PAIR, PAIR)],
            w_v.at[pair, rows, pl.ds(kind * PAIR, PAIR)],
            ld_sem.at[sem],
        )

    def first_loads(i):
        part = pl.ds(pl.multiple_of(i * PART, PART), PART)
        return (
            pltpu.make_async_copy(
                mem_hbm.at[0, :, part], states.at[0, :, part], ld_sem.at[i]
            ),
            load_w(wk_hbm, 0, 0, i, PART, 4 + i),
        )

    load_v0 = load_w(wv_hbm, 0, 1, 0, D, 8)

    load_kv1 = (
        load_w(wk_hbm, 1, 0, 0, D, 12),
        load_w(wv_hbm, 1, 1, 0, D, 13),
    )
    load_lens = pltpu.make_async_copy(lens_hbm, lens, ld_sem.at[17])
    load_x = pltpu.make_async_copy(x_hbm.at[0], states.at[1], ld_sem.at[14])
    load_q = pltpu.make_async_copy(wq_hbm, w_v.at[2], ld_sem.at[15])
    load_wo = pltpu.make_async_copy(wo_hbm, wo_v, ld_sem.at[16])
    for i in range(2):
        for copy in first_loads(i):
            copy.start()
    load_lens.start()

    def remote(src, dst, send, recv, to):
        return pltpu.make_async_remote_copy(
            src_ref=src,
            dst_ref=dst,
            send_sem=send,
            recv_sem=recv,
            device_id=to,
            device_id_type=MESH,
        )

    def kv_copy(c):
        return remote(kv_send.at[c], kv_recv.at[c], kvs.at[c], kvr.at[c], following)

    def tile(zz, cc):
        return lax.rem(zz + 4, 4) * 2 + cc

    half = COLS // 2

    def cross_copy(i):
        g = tile(z + 2 * (i // 2), core)
        rows = pl.ds((i % 2) * half, half)
        return remote(
            wo_hbm.at[rows, pl.ds(pl.multiple_of(g * TW, TW), TW)],
            wof.at[g, rows],
            wcs.at[i],
            wcr.at[i],
            cross,
        )

    def z_copy(by, i, zz):
        g = tile(zz, core)
        rows = pl.ds(i * half, half)
        k = (1 - by) + i
        return remote(
            wof.at[g, rows], wof.at[g, rows], wzs.at[k], wzr.at[k], along_z(by)
        )

    def sibling_copy(i, cc):
        g = tile(z + (0, 1, -1, 2)[i], cc)
        return remote(wof.at[g], wof.at[g], wbs.at[i], wbr.at[i], sibling)

    load_lens.wait()
    own_len = lens[s]
    mem_len = lens[lax.rem(s + 15, 16)]

    def row_start(d, which):
        return (lax.rem(x + d, 4) * 2 + which) * 64

    def at_column(c):
        return c if isinstance(c, int) else pl.multiple_of(c, HD)

    def attend(pairs, group):
        which = 1 - yh + group * (2 * yh - 1)
        starts = [row_start(d, which) for d in D_ORDER]
        rows = [pl.ds(pl.multiple_of(start, 64), 64) for start in starts]
        ids = jnp.concatenate(
            [lax.broadcasted_iota(jnp.int32, (64, 1), 0) + start for start in starts],
            axis=0,
        )
        last = jnp.minimum(ids, own_len - 1)
        col = lax.broadcasted_iota(jnp.int32, (1, SEG), 1)
        ones = jnp.ones((SEG, HD), BF16)
        for pair, hh in [(pair, hh) for pair in pairs for hh in range(2)]:
            ks = slice(hh * HD, (hh + 1) * HD)
            vs = slice(PAIR + hh * HD, PAIR + (hh + 1) * HD)
            qs = pl.ds(at_column(pair * PAIR + hh * HD), HD)
            q = jnp.concatenate([made[2, r, qs] for r in rows], axis=0)
            dims = (((1,), (1,)), ((), ()))
            s_mem = SCALE * lax.dot_general(
                q, kv_recv[2 * pair, :, ks], dims, preferred_element_type=F32
            )
            s_own = SCALE * lax.dot_general(
                q, made[3 + pair, :, ks], dims, preferred_element_type=F32
            )
            s_mem = jnp.concatenate(
                [
                    s_mem[:, :256],
                    jnp.where(col[:, 256:] < mem_len, s_mem[:, 256:], MASKED),
                ],
                axis=1,
            )
            s_own = jnp.where(col <= last, s_own, MASKED)
            top = jnp.max(jnp.maximum(s_mem, s_own), axis=1, keepdims=True)
            w_mem = jnp.exp2(s_mem - top).astype(BF16)
            w_own = jnp.exp2(s_own - top).astype(BF16)
            v_mem = jnp.concatenate([kv_recv[2 * pair + 1, :, ks], ones], axis=1)
            v_own = jnp.concatenate([made[3 + pair, :, vs], ones], axis=1)
            r = jnp.dot(w_mem, v_mem, preferred_element_type=F32) + jnp.dot(
                w_own, v_own, preferred_element_type=F32
            )
            ctx[group * 2 + pair, :, ks] = (r[:, :HD] / r[:, HD:]).astype(BF16)

    def ctx_copy(pair):
        return remote(
            ctx.at[pair], ctx_recv.at[pair], cxs.at[pair], cxr.at[pair], partner
        )

    def first_part(i, _):
        c = i // 4
        n = lax.rem(i, 4)

        @pl.when(i < 4)
        def _():
            for copy in first_loads(n):
                copy.wait()

        @pl.when(i < 2)
        def _():
            for copy in first_loads(n + 2):
                copy.start()

        @pl.when(i == 2)
        def _():
            load_v0.start()

        @pl.when(i == 4)
        def _():
            load_v0.wait()
            load_kv1[0].start()
            load_kv1[1].start()

        part = pl.ds(pl.multiple_of(n * PART, PART), PART)
        cols = pl.ds(pl.multiple_of(c * PAIR, PAIR), PAIR)
        term = jnp.dot(
            states[0, :, part], w_v[0, part, cols], preferred_element_type=F32
        )

        @pl.when(n == 0)
        def _():
            first[...] = term

        @pl.when(n > 0)
        def _():
            first[...] += term

        @pl.when(n == 3)
        def _():
            kv_send[c] = first[...].astype(BF16)

        @pl.when(i == 3)
        def _():
            pl.semaphore_wait(barrier, 8)

        @pl.when(n == 3)
        def _():
            kv_copy(c).start()

        @pl.when(i == 3)
        def _():
            cross_copy(0).start()
            cross_copy(1).start()

        return 0

    lax.fori_loop(0, 8, first_part, 0)

    def make(i, _):
        own_part = jnp.minimum(i // 2, 1)
        w = lax.rem(i, 3)

        @pl.when(i == 1)
        def _():
            load_x.start()
            load_q.start()
            load_kv1[0].wait()
            load_kv1[1].wait()

        @pl.when(i == 2)
        def _():
            load_x.wait()
            load_q.wait()
            load_wo.start()

        made[i] = jnp.dot(
            states[own_part], w_v[w], preferred_element_type=F32
        ).astype(BF16)

        @pl.when(i == 1)
        def _():
            for c in range(2):
                kv_send[2 + c] = made[1, :, c * PAIR : (c + 1) * PAIR]
                kv_copy(2 + c).start()

        @pl.when(i == 3)
        def _():
            cross_copy(0).wait_recv()
            z_copy(1, 0, z).start()
            z_copy(-1, 0, z).start()

        @pl.when(i == 4)
        def _():
            cross_copy(1).wait_recv()
            z_copy(1, 1, z).start()
            z_copy(-1, 1, z).start()
            sibling_copy(0, core).start()
            cross_copy(2).start()

        return 0

    def phase(ph, _):
        lax.fori_loop(1 + 3 * ph, 4 + ph, make, 0)
        kv_copy(2 * ph).wait_recv()
        kv_copy(2 * ph + 1).wait_recv()
        attend((ph,), 0)
        ctx_copy(ph).start()
        return 0

    lax.fori_loop(0, 2, phase, 0)
    cross_copy(3).start()
    attend((0, 1), 1)
    load_wo.wait()

    def both_pairs(ref, at_pair):
        return jnp.concatenate([ref[at_pair], ref[at_pair + 1]], axis=1)

    def local_step(i, _):
        cols = pl.ds(pl.multiple_of(i * 1024, 1024), 1024)
        p_loc[:, cols] = jnp.dot(
            both_pairs(ctx, 2), wo_v[:, cols], preferred_element_type=F32
        )
        return 0

    lax.fori_loop(0, 4, local_step, 0)
    ctx_copy(0).wait_recv()
    ctx_copy(1).wait_recv()

    def tile_of(k):
        j = k // 2
        off = j + j // 2 - 2 * (j // 3)
        par = lax.rem(k, 2)
        return tile(z + off, core + par * (1 - 2 * core))

    def far_copy(k):
        sgn = 1 - 2 * lax.rem(k, 2)
        return remote(
            p_buf.at[k, pl.ds(0, 64)], r1.at[k], r1s.at[k], r1r.at[k], along_x(sgn)
        )

    def back_copy(k):
        par = lax.rem(k, 2)
        rows = pl.ds(pl.multiple_of(128 - 64 * par, 64), 64)
        return remote(
            p_buf.at[k, rows], rb.at[k], rbs.at[k], rbr.at[k], along_x(2 * par - 1)
        )

    def fwd_rows(k):
        return pl.ds(pl.multiple_of(64 + 64 * lax.rem(k, 2), 64), 64)

    def fwd_copy(k):
        return remote(
            p_buf.at[k, fwd_rows(k)],
            rf.at[k],
            rfs.at[k],
            rfr.at[k],
            along_x(1 - 2 * lax.rem(k, 2)),
        )

    def project_tile(k):
        g = tile_of(k)
        cols = pl.ds(pl.multiple_of(g * TW, TW), TW)
        acc = p_loc[:, cols] + jnp.dot(
            both_pairs(ctx_recv, 0), wof[g], preferred_element_type=F32
        )
        p_buf[k] = acc.astype(BF16)
        far_copy(k).start()
        back_copy(k).start()

    def combine(k):
        far_copy(k).wait_recv()
        rows = fwd_rows(k)
        p_buf[k, rows] = (p_buf[k, rows].astype(F32) + r1[k].astype(F32)).astype(BF16)
        fwd_copy(k).start()

    def finish(k):
        back_copy(k).wait_recv()
        fwd_copy(k).wait_recv()
        g = tile_of(k)
        cols = pl.ds(pl.multiple_of(g * TW, TW), TW)
        out_ref[:, cols] = (
            p_buf[k, 192:256].astype(F32) + rb[k].astype(F32) + rf[k].astype(F32)
        ).astype(BF16)

    def out_step(k, _):
        for j in range(4):

            @pl.when(k == 2 * j)
            def _(j=j):
                if j == 1:
                    z_copy(-1, 0, z + 1).wait_recv()
                    z_copy(-1, 1, z + 1).wait_recv()
                if j == 2:
                    z_copy(1, 0, z - 1).wait_recv()
                    z_copy(1, 1, z - 1).wait_recv()
                if j == 3:
                    cross_copy(2).wait_recv()
                    cross_copy(3).wait_recv()
                if j > 0:
                    sibling_copy(j, core).start()

            @pl.when(k == 2 * j + 1)
            def _(j=j):
                sibling_copy(j, 1 - core).wait_recv()

        @pl.when(k < NT)
        def _():
            project_tile(k)

        @pl.when(k >= 4)
        def _():
            combine(k - 4)

        return 0

    lax.fori_loop(0, NT + 4, out_step, 0)

    def last_step(k, _):
        finish(k)
        return 0

    lax.fori_loop(0, NT, last_step, 0)

    for c in range(4):
        sibling_copy(c, core).wait_send()
        cross_copy(c).wait_send()
        kv_copy(c).wait_send()
    for pair in range(2):
        ctx_copy(pair).wait_send()
    for i in range(2):
        z_copy(1, i, z).wait_send()
        z_copy(-1, i, z).wait_send()

    def drain(k, _):
        far_copy(k).wait_send()
        back_copy(k).wait_send()
        fwd_copy(k).wait_send()
        return 0

    lax.fori_loop(0, NT, drain, 0)


def body(layer_input, memory, seg_lengths, query_weight, key_weight, value_weight, out_weight):
    dma = pltpu.SemaphoreType.DMA
    out = pl.pallas_call(
        kernel,
        out_shape=jax.ShapeDtypeStruct((64, D), BF16),
        in_specs=[pl.BlockSpec(memory_space=pltpu.HBM)] * 7,
        out_specs=pl.BlockSpec(memory_space=pltpu.VMEM),
        scratch_shapes=[
            pltpu.SMEM((16,), jnp.int32),
            pltpu.VMEM((2, SEG, D), BF16),
            pltpu.VMEM((3, D, COLS), BF16),
            pltpu.VMEM((COLS, D), BF16),
            pltpu.VMEM((NT, COLS, TW), BF16),
            pltpu.VMEM((4, SEG, PAIR), BF16),
            pltpu.VMEM((4, SEG, PAIR), BF16),
            pltpu.VMEM((5, SEG, COLS), BF16),
            pltpu.VMEM((4, 256, PAIR), BF16),
            pltpu.VMEM((2, 256, PAIR), BF16),
            pltpu.VMEM((SEG, PAIR), F32),
            pltpu.VMEM((256, D), F32),
            pltpu.VMEM((NT, 256, TW), BF16),
            pltpu.VMEM((NT, 64, TW), BF16),
            pltpu.VMEM((NT, 64, TW), BF16),
            pltpu.VMEM((NT, 64, TW), BF16),
            dma((18,)),
            dma((4,)),
            dma((4,)),
            dma((2,)),
            dma((2,)),
            dma((4,)),
            dma((4,)),
            dma((4,)),
            dma((4,)),
            dma((4,)),
            dma((4,)),
            dma((NT,)),
            dma((NT,)),
            dma((NT,)),
            dma((NT,)),
            dma((NT,)),
            dma((NT,)),
        ],
        compiler_params=pltpu.CompilerParams(
            collective_id=0, has_side_effects=True, vmem_limit_bytes=50 * 2**20
        ),
    )(
        seg_lengths,
        layer_input,
        memory,
        query_weight,
        key_weight,
        value_weight,
        out_weight,
    )
    return out[None]


def solution(mesh):
    return jax.shard_map(
        body,
        mesh=mesh,
        in_specs=(
            P("seq", None, None),
            P("seq", None, None),
            P(),
            P(None, "tp"),
            P(None, "tp"),
            P(None, "tp"),
            P("tp", None),
        ),
        out_specs=P("seq", "tp", None),
        check_vma=False,
    )
```

```python
import functools
import math

import jax
import jax.numpy as jnp
from jax import lax
from jax.experimental import pallas as pl
from jax.experimental.pallas import tpu as pltpu
from jax.sharding import PartitionSpec as P

F32 = jnp.float32
BF16 = jnp.bfloat16
MESH = pl.DeviceIdType.MESH

SEG = 512
D = 4096
HD = 128
COLS = 512
PAIR = 256
PART = 2048
TW = 512
NT = D // TW
SCALE = math.log2(math.e) / math.sqrt(HD)
MASKED = -3e38
D_ORDER = (2, 1, 3, 0)


def kernel(
    lens_hbm,
    x_hbm,
    mem_hbm,
    wq_hbm,
    wk_hbm,
    wv_hbm,
    wo_hbm,
    out_ref,
    lens,
    states,
    w_v,
    wo_v,
    wof,
    kv_send,
    kv_recv,
    made,
    ctx,
    ctx_recv,
    first,
    p_loc,
    p_buf,
    r1,
    rb,
    rf,
    ld_sem,
    kvs,
    kvr,
    cxs,
    cxr,
    wcs,
    wcr,
    wzs,
    wzr,
    wbs,
    wbr,
    r1s,
    r1r,
    rbs,
    rbr,
    rfs,
    rfr,
):
    s = lax.axis_index("seq")
    t = lax.axis_index("tp")
    core = lax.rem(s, 2)
    yl = lax.rem(s // 2, 2)
    z = s // 4
    x = t // 2
    yh = lax.rem(t, 2)

    def at(seq, tp):
        return {"seq": seq, "tp": tp}

    following = at(lax.rem(s + 1, 16), t)
    previous = at(lax.rem(s + 15, 16), t)
    partner = at(s, x * 2 + 1 - yh)
    cross = at(z * 4 + (1 - yl) * 2 + core, x * 2 + 1 - yh)
    sibling = at(s + 1 - 2 * core, t)

    def along_z(by):
        return at(lax.rem(z + by + 4, 4) * 4 + yl * 2 + core, t)

    def along_x(by):
        return at(s, lax.rem(x + by + 4, 4) * 2 + yh)

    def load_w(src, pair, kind, part, depth, sem):
        rows = pl.ds(part * depth, depth)
        return pltpu.make_async_copy(
            src.at[rows, pl.ds(pair * PAIR, PAIR)],
            w_v.at[pair, rows, pl.ds(kind * PAIR, PAIR)],
            ld_sem.at[sem],
        )

    def first_loads(i):
        part = pl.ds(pl.multiple_of(i * PART, PART), PART)
        return (
            pltpu.make_async_copy(
                mem_hbm.at[0, :, part], states.at[0, :, part], ld_sem.at[i]
            ),
            load_w(wk_hbm, 0, 0, i, PART, 4 + i),
        )

    load_v0 = load_w(wv_hbm, 0, 1, 0, D, 8)

    load_kv1 = (
        load_w(wk_hbm, 1, 0, 0, D, 12),
        load_w(wv_hbm, 1, 1, 0, D, 13),
    )
    load_lens = pltpu.make_async_copy(lens_hbm, lens, ld_sem.at[17])
    load_x = pltpu.make_async_copy(x_hbm.at[0], states.at[1], ld_sem.at[14])
    load_q = pltpu.make_async_copy(wq_hbm, w_v.at[2], ld_sem.at[15])
    load_wo = pltpu.make_async_copy(wo_hbm, wo_v, ld_sem.at[16])
    for i in range(2):
        for copy in first_loads(i):
            copy.start()
    load_lens.start()

    barrier = pltpu.get_barrier_semaphore()
    for peer in (
        following,
        previous,
        partner,
        cross,
        along_z(1),
        along_z(-1),
        along_x(1),
        along_x(-1),
    ):
        pl.semaphore_signal(barrier, inc=1, device_id=peer, device_id_type=MESH)

    def remote(src, dst, send, recv, to):
        return pltpu.make_async_remote_copy(
            src_ref=src,
            dst_ref=dst,
            send_sem=send,
            recv_sem=recv,
            device_id=to,
            device_id_type=MESH,
        )

    def kv_copy(c):
        return remote(kv_send.at[c], kv_recv.at[c], kvs.at[c], kvr.at[c], following)

    def tile(zz, cc):
        return lax.rem(zz + 4, 4) * 2 + cc

    half = COLS // 2

    def cross_copy(i):
        g = tile(z + 2 * (i // 2), core)
        rows = pl.ds((i % 2) * half, half)
        return remote(
            wo_hbm.at[rows, pl.ds(pl.multiple_of(g * TW, TW), TW)],
            wof.at[g, rows],
            wcs.at[i],
            wcr.at[i],
            cross,
        )

    def z_copy(by, i, zz):
        g = tile(zz, core)
        rows = pl.ds(i * half, half)
        k = (1 - by) + i
        return remote(
            wof.at[g, rows], wof.at[g, rows], wzs.at[k], wzr.at[k], along_z(by)
        )

    def sibling_copy(i, cc):
        g = tile(z + (0, 1, -1, 2)[i], cc)
        return remote(wof.at[g], wof.at[g], wbs.at[i], wbr.at[i], sibling)


    def row_start(d, which):
        return (lax.rem(x + d, 4) * 2 + which) * 64

    def at_column(c):
        return c if isinstance(c, int) else pl.multiple_of(c, HD)

    def attend(pairs, group):
        which = 1 - yh + group * (2 * yh - 1)
        starts = [row_start(d, which) for d in D_ORDER]
        rows = [pl.ds(pl.multiple_of(start, 64), 64) for start in starts]
        ids = jnp.concatenate(
            [lax.broadcasted_iota(jnp.int32, (64, 1), 0) + start for start in starts],
            axis=0,
        )
        col = lax.broadcasted_iota(jnp.int32, (1, SEG), 1)
        ones = jnp.ones((SEG, HD), BF16)
        own_len = lens[s]
        mem_len = lens[lax.rem(s + 15, 16)]
        last = jnp.minimum(ids, own_len - 1)
        for pair, hh in [(pair, hh) for pair in pairs for hh in range(2)]:
            ks = slice(hh * HD, (hh + 1) * HD)
            vs = slice(PAIR + hh * HD, PAIR + (hh + 1) * HD)
            qs = pl.ds(at_column(pair * PAIR + hh * HD), HD)
            q = jnp.concatenate([made[2, r, qs] for r in rows], axis=0)
            dims = (((1,), (1,)), ((), ()))
            s_mem = SCALE * lax.dot_general(
                q, kv_recv[2 * pair, :, ks], dims, preferred_element_type=F32
            )
            s_own = SCALE * lax.dot_general(
                q, made[3 + pair, :, ks], dims, preferred_element_type=F32
            )
            s_mem = jnp.concatenate(
                [
                    s_mem[:, :256],
                    jnp.where(col[:, 256:] < mem_len, s_mem[:, 256:], MASKED),
                ],
                axis=1,
            )
            s_own = jnp.where(col <= last, s_own, MASKED)
            top = jnp.max(jnp.maximum(s_mem, s_own), axis=1, keepdims=True)
            w_mem = jnp.exp2(s_mem - top).astype(BF16)
            w_own = jnp.exp2(s_own - top).astype(BF16)
            v_mem = jnp.concatenate([kv_recv[2 * pair + 1, :, ks], ones], axis=1)
            v_own = jnp.concatenate([made[3 + pair, :, vs], ones], axis=1)
            r = jnp.dot(w_mem, v_mem, preferred_element_type=F32) + jnp.dot(
                w_own, v_own, preferred_element_type=F32
            )
            ctx[group * 2 + pair, :, ks] = (r[:, :HD] / r[:, HD:]).astype(BF16)

    def ctx_copy(pair):
        return remote(
            ctx.at[pair], ctx_recv.at[pair], cxs.at[pair], cxr.at[pair], partner
        )

    def first_part(i, _):
        c = i // 2
        n = lax.rem(i, 2)

        @pl.when(i < 2)
        def _():
            for copy in first_loads(n):
                copy.wait()

        @pl.when(i == 0)
        def _():
            load_v0.start()

        @pl.when(i == 2)
        def _():
            load_v0.wait()
            load_kv1[0].start()
            load_kv1[1].start()

        part = pl.ds(pl.multiple_of(n * PART, PART), PART)
        cols = pl.ds(pl.multiple_of(c * PAIR, PAIR), PAIR)
        term = jnp.dot(
            states[0, :, part], w_v[0, part, cols], preferred_element_type=F32
        )

        @pl.when(n == 0)
        def _():
            first[...] = term

        @pl.when(n > 0)
        def _():
            first[...] += term

        @pl.when(n == 1)
        def _():
            kv_send[c] = first[...].astype(BF16)

        @pl.when(i == 1)
        def _():
            pl.semaphore_wait(barrier, 8)

        @pl.when(n == 1)
        def _():
            kv_copy(c).start()

        @pl.when(i == 1)
        def _():
            cross_copy(0).start()
            cross_copy(1).start()

        return 0

    lax.fori_loop(0, 4, first_part, 0)

    def make(i, _):
        own_part = jnp.minimum(i // 2, 1)
        w = lax.rem(i, 3)

        @pl.when(i == 1)
        def _():
            load_x.start()
            load_q.start()
            load_kv1[0].wait()
            load_kv1[1].wait()

        @pl.when(i == 2)
        def _():
            load_x.wait()
            load_q.wait()
            load_wo.start()

        made[i] = jnp.dot(
            states[own_part], w_v[w], preferred_element_type=F32
        ).astype(BF16)

        @pl.when(i == 1)
        def _():
            for c in range(2):
                kv_send[2 + c] = made[1, :, c * PAIR : (c + 1) * PAIR]
                kv_copy(2 + c).start()

        @pl.when(i == 3)
        def _():
            cross_copy(0).wait_recv()
            z_copy(1, 0, z).start()
            z_copy(-1, 0, z).start()

        @pl.when(i == 4)
        def _():
            cross_copy(1).wait_recv()
            z_copy(1, 1, z).start()
            z_copy(-1, 1, z).start()
            sibling_copy(0, core).start()
            cross_copy(2).start()

        return 0

    def phase(ph, _):
        lax.fori_loop(1 + 3 * ph, 4 + ph, make, 0)
        kv_copy(2 * ph).wait_recv()
        kv_copy(2 * ph + 1).wait_recv()
        attend((ph,), 0)
        ctx_copy(ph).start()
        return 0

    load_lens.wait()
    lax.fori_loop(0, 2, phase, 0)
    cross_copy(3).start()
    attend((0, 1), 1)
    load_wo.wait()

    def both_pairs(ref, at_pair):
        return jnp.concatenate([ref[at_pair], ref[at_pair + 1]], axis=1)

    def local_step(i, _):
        cols = pl.ds(pl.multiple_of(i * 1024, 1024), 1024)
        p_loc[:, cols] = jnp.dot(
            both_pairs(ctx, 2), wo_v[:, cols], preferred_element_type=F32
        )
        return 0

    lax.fori_loop(0, 4, local_step, 0)
    ctx_copy(0).wait_recv()
    ctx_copy(1).wait_recv()

    def tile_of(k):
        j = k // 2
        off = j + j // 2 - 2 * (j // 3)
        par = lax.rem(k, 2)
        return tile(z + off, core + par * (1 - 2 * core))

    def far_copy(k):
        sgn = 1 - 2 * lax.rem(k, 2)
        return remote(
            p_buf.at[k, pl.ds(0, 64)], r1.at[k], r1s.at[k], r1r.at[k], along_x(sgn)
        )

    def back_copy(k):
        par = lax.rem(k, 2)
        rows = pl.ds(pl.multiple_of(128 - 64 * par, 64), 64)
        return remote(
            p_buf.at[k, rows], rb.at[k], rbs.at[k], rbr.at[k], along_x(2 * par - 1)
        )

    def fwd_rows(k):
        return pl.ds(pl.multiple_of(64 + 64 * lax.rem(k, 2), 64), 64)

    def fwd_copy(k):
        return remote(
            p_buf.at[k, fwd_rows(k)],
            rf.at[k],
            rfs.at[k],
            rfr.at[k],
            along_x(1 - 2 * lax.rem(k, 2)),
        )

    def project_tile(k):
        g = tile_of(k)
        cols = pl.ds(pl.multiple_of(g * TW, TW), TW)
        acc = p_loc[:, cols] + jnp.dot(
            both_pairs(ctx_recv, 0), wof[g], preferred_element_type=F32
        )
        p_buf[k] = acc.astype(BF16)
        far_copy(k).start()
        back_copy(k).start()

    def combine(k):
        far_copy(k).wait_recv()
        rows = fwd_rows(k)
        p_buf[k, rows] = (p_buf[k, rows].astype(F32) + r1[k].astype(F32)).astype(BF16)
        fwd_copy(k).start()

    def finish(k):
        back_copy(k).wait_recv()
        fwd_copy(k).wait_recv()
        g = tile_of(k)
        cols = pl.ds(pl.multiple_of(g * TW, TW), TW)
        out_ref[:, cols] = (
            p_buf[k, 192:256].astype(F32) + rb[k].astype(F32) + rf[k].astype(F32)
        ).astype(BF16)

    def out_step(k, _):
        @pl.when(k >= 3)
        def _():
            combine(k - 3)

        for j in range(4):

            @pl.when(k == 2 * j)
            def _(j=j):
                if j == 1:
                    z_copy(-1, 0, z + 1).wait_recv()
                    z_copy(-1, 1, z + 1).wait_recv()
                if j == 2:
                    z_copy(1, 0, z - 1).wait_recv()
                    z_copy(1, 1, z - 1).wait_recv()
                if j == 3:
                    cross_copy(2).wait_recv()
                    cross_copy(3).wait_recv()
                if j > 0:
                    sibling_copy(j, core).start()

            @pl.when(k == 2 * j + 1)
            def _(j=j):
                sibling_copy(j, 1 - core).wait_recv()

        @pl.when(k < NT)
        def _():
            project_tile(k)

        return 0

    lax.fori_loop(0, NT + 3, out_step, 0)

    def last_step(k, _):
        finish(k)
        return 0

    lax.fori_loop(0, NT, last_step, 0)

    for c in range(4):
        sibling_copy(c, core).wait_send()
        cross_copy(c).wait_send()
        kv_copy(c).wait_send()
    for pair in range(2):
        ctx_copy(pair).wait_send()
    for i in range(2):
        z_copy(1, i, z).wait_send()
        z_copy(-1, i, z).wait_send()

    def drain(k, _):
        far_copy(k).wait_send()
        back_copy(k).wait_send()
        fwd_copy(k).wait_send()
        return 0

    lax.fori_loop(0, NT, drain, 0)


def body(layer_input, memory, seg_lengths, query_weight, key_weight, value_weight, out_weight):
    dma = pltpu.SemaphoreType.DMA
    out = pl.pallas_call(
        kernel,
        out_shape=jax.ShapeDtypeStruct((64, D), BF16),
        in_specs=[pl.BlockSpec(memory_space=pltpu.HBM)] * 7,
        out_specs=pl.BlockSpec(memory_space=pltpu.VMEM),
        scratch_shapes=[
            pltpu.SMEM((16,), jnp.int32),
            pltpu.VMEM((2, SEG, D), BF16),
            pltpu.VMEM((3, D, COLS), BF16),
            pltpu.VMEM((COLS, D), BF16),
            pltpu.VMEM((NT, COLS, TW), BF16),
            pltpu.VMEM((4, SEG, PAIR), BF16),
            pltpu.VMEM((4, SEG, PAIR), BF16),
            pltpu.VMEM((5, SEG, COLS), BF16),
            pltpu.VMEM((4, 256, PAIR), BF16),
            pltpu.VMEM((2, 256, PAIR), BF16),
            pltpu.VMEM((SEG, PAIR), F32),
            pltpu.VMEM((256, D), F32),
            pltpu.VMEM((NT, 256, TW), BF16),
            pltpu.VMEM((NT, 64, TW), BF16),
            pltpu.VMEM((NT, 64, TW), BF16),
            pltpu.VMEM((NT, 64, TW), BF16),
            dma((18,)),
            dma((4,)),
            dma((4,)),
            dma((2,)),
            dma((2,)),
            dma((4,)),
            dma((4,)),
            dma((4,)),
            dma((4,)),
            dma((4,)),
            dma((4,)),
            dma((NT,)),
            dma((NT,)),
            dma((NT,)),
            dma((NT,)),
            dma((NT,)),
            dma((NT,)),
        ],
        compiler_params=pltpu.CompilerParams(
            collective_id=0, has_side_effects=True, vmem_limit_bytes=50 * 2**20
        ),
    )(
        seg_lengths,
        layer_input,
        memory,
        query_weight,
        key_weight,
        value_weight,
        out_weight,
    )
    return out[None]


def solution(mesh):
    return jax.shard_map(
        body,
        mesh=mesh,
        in_specs=(
            P("seq", None, None),
            P("seq", None, None),
            P(),
            P(None, "tp"),
            P(None, "tp"),
            P(None, "tp"),
            P("tp", None),
        ),
        out_specs=P("seq", "tp", None),
        check_vma=False,
    )
```

```python
import functools
import math

import jax
import jax.numpy as jnp
from jax import lax
from jax.experimental import pallas as pl
from jax.experimental.pallas import tpu as pltpu
from jax.sharding import PartitionSpec as P

F32 = jnp.float32
BF16 = jnp.bfloat16
MESH = pl.DeviceIdType.MESH

SEG = 512
D = 4096
HD = 128
COLS = 512
PAIR = 256
PART = 2048
TW = 512
NT = D // TW
SCALE = math.log2(math.e) / math.sqrt(HD)
MASKED = -3e38
D_ORDER = (2, 1, 3, 0)


def kernel(
    lens_hbm,
    x_hbm,
    mem_hbm,
    wq_hbm,
    wk_hbm,
    wv_hbm,
    wo_hbm,
    out_ref,
    lens,
    states,
    w_v,
    wo_v,
    wof,
    kv_send,
    kv_recv,
    made,
    ctx,
    ctx_recv,
    first,
    p_loc,
    p_buf,
    r1,
    rb,
    rf,
    ld_sem,
    kvs,
    kvr,
    cxs,
    cxr,
    wcs,
    wcr,
    wzs,
    wzr,
    wbs,
    wbr,
    r1s,
    r1r,
    rbs,
    rbr,
    rfs,
    rfr,
):
    s = lax.axis_index("seq")
    t = lax.axis_index("tp")
    core = lax.rem(s, 2)
    yl = lax.rem(s // 2, 2)
    z = s // 4
    x = t // 2
    yh = lax.rem(t, 2)

    def at(seq, tp):
        return {"seq": seq, "tp": tp}

    following = at(lax.rem(s + 1, 16), t)
    previous = at(lax.rem(s + 15, 16), t)
    partner = at(s, x * 2 + 1 - yh)
    cross = at(z * 4 + (1 - yl) * 2 + core, x * 2 + 1 - yh)
    sibling = at(s + 1 - 2 * core, t)

    def along_z(by):
        return at(lax.rem(z + by + 4, 4) * 4 + yl * 2 + core, t)

    def along_x(by):
        return at(s, lax.rem(x + by + 4, 4) * 2 + yh)

    def load_w(src, pair, kind, part, depth, sem):
        rows = pl.ds(part * depth, depth)
        return pltpu.make_async_copy(
            src.at[rows, pl.ds(pair * PAIR, PAIR)],
            w_v.at[pair, rows, pl.ds(kind * PAIR, PAIR)],
            ld_sem.at[sem],
        )

    def first_loads(i):
        part = pl.ds(pl.multiple_of(i * PART, PART), PART)
        return (
            pltpu.make_async_copy(
                mem_hbm.at[0, :, part], states.at[0, :, part], ld_sem.at[i]
            ),
            load_w(wk_hbm, 0, 0, i, PART, 4 + i),
        )

    load_v0 = load_w(wv_hbm, 0, 1, 0, D, 8)

    load_kv1 = (
        load_w(wk_hbm, 1, 0, 0, D, 12),
        load_w(wv_hbm, 1, 1, 0, D, 13),
    )
    load_lens = pltpu.make_async_copy(lens_hbm, lens, ld_sem.at[17])
    load_x = pltpu.make_async_copy(x_hbm.at[0], states.at[1], ld_sem.at[14])
    load_q = pltpu.make_async_copy(wq_hbm, w_v.at[2], ld_sem.at[15])
    load_wo = pltpu.make_async_copy(wo_hbm, wo_v, ld_sem.at[16])
    for i in range(2):
        for copy in first_loads(i):
            copy.start()
    load_lens.start()

    barrier = pltpu.get_barrier_semaphore()
    for peer in (
        following,
        previous,
        partner,
        cross,
        along_z(1),
        along_z(-1),
        along_x(1),
        along_x(-1),
    ):
        pl.semaphore_signal(barrier, inc=1, device_id=peer, device_id_type=MESH)

    def remote(src, dst, send, recv, to):
        return pltpu.make_async_remote_copy(
            src_ref=src,
            dst_ref=dst,
            send_sem=send,
            recv_sem=recv,
            device_id=to,
            device_id_type=MESH,
        )

    def kv_copy(c):
        return remote(kv_send.at[c], kv_recv.at[c], kvs.at[c], kvr.at[c], following)

    def tile(zz, cc):
        return lax.rem(zz + 4, 4) * 2 + cc

    half = COLS // 2

    def cross_copy(i):
        g = tile(z + 2 * (i // 2), core)
        rows = pl.ds((i % 2) * half, half)
        return remote(
            wo_hbm.at[rows, pl.ds(pl.multiple_of(g * TW, TW), TW)],
            wof.at[g, rows],
            wcs.at[i],
            wcr.at[i],
            cross,
        )

    def z_copy(by, i, zz):
        g = tile(zz, core)
        rows = pl.ds(i * half, half)
        k = (1 - by) + i
        return remote(
            wof.at[g, rows], wof.at[g, rows], wzs.at[k], wzr.at[k], along_z(by)
        )

    def sibling_copy(i, cc):
        g = tile(z + (0, 1, -1, 2)[i], cc)
        return remote(wof.at[g], wof.at[g], wbs.at[i], wbr.at[i], sibling)


    def row_start(d, which):
        return (lax.rem(x + d, 4) * 2 + which) * 64

    def at_column(c):
        return c if isinstance(c, int) else pl.multiple_of(c, HD)

    def attend(pairs, group):
        which = 1 - yh + group * (2 * yh - 1)
        starts = [row_start(d, which) for d in D_ORDER]
        rows = [pl.ds(pl.multiple_of(start, 64), 64) for start in starts]
        ids = jnp.concatenate(
            [lax.broadcasted_iota(jnp.int32, (64, 1), 0) + start for start in starts],
            axis=0,
        )
        col = lax.broadcasted_iota(jnp.int32, (1, SEG), 1)
        ones = jnp.ones((SEG, HD), BF16)
        own_len = lens[s]
        mem_len = lens[lax.rem(s + 15, 16)]
        last = jnp.minimum(ids, own_len - 1)
        for pair, hh in [(pair, hh) for pair in pairs for hh in range(2)]:
            ks = slice(hh * HD, (hh + 1) * HD)
            vs = slice(PAIR + hh * HD, PAIR + (hh + 1) * HD)
            qs = pl.ds(at_column(pair * PAIR + hh * HD), HD)
            q = jnp.concatenate([made[2, r, qs] for r in rows], axis=0)
            dims = (((1,), (1,)), ((), ()))
            s_mem = SCALE * lax.dot_general(
                q, kv_recv[2 * pair, :, ks], dims, preferred_element_type=F32
            )
            s_own = SCALE * lax.dot_general(
                q, made[3 + pair, :, ks], dims, preferred_element_type=F32
            )
            s_mem = jnp.concatenate(
                [
                    s_mem[:, :256],
                    jnp.where(col[:, 256:] < mem_len, s_mem[:, 256:], MASKED),
                ],
                axis=1,
            )
            s_own = jnp.where(col <= last, s_own, MASKED)
            top = jnp.max(jnp.maximum(s_mem, s_own), axis=1, keepdims=True)
            w_mem = jnp.exp2(s_mem - top).astype(BF16)
            w_own = jnp.exp2(s_own - top).astype(BF16)
            v_mem = jnp.concatenate([kv_recv[2 * pair + 1, :, ks], ones], axis=1)
            v_own = jnp.concatenate([made[3 + pair, :, vs], ones], axis=1)
            r = jnp.dot(w_mem, v_mem, preferred_element_type=F32) + jnp.dot(
                w_own, v_own, preferred_element_type=F32
            )
            ctx[group * 2 + pair, :, ks] = (r[:, :HD] / r[:, HD:]).astype(BF16)

    def ctx_copy(pair):
        return remote(
            ctx.at[pair], ctx_recv.at[pair], cxs.at[pair], cxr.at[pair], partner
        )

    def first_part(i, _):
        c = i // 2
        n = lax.rem(i, 2)

        @pl.when(i < 2)
        def _():
            for copy in first_loads(n):
                copy.wait()

        @pl.when(i == 0)
        def _():
            load_v0.start()

        @pl.when(i == 2)
        def _():
            load_v0.wait()
            load_kv1[0].start()
            load_kv1[1].start()

        part = pl.ds(pl.multiple_of(n * PART, PART), PART)
        cols = pl.ds(pl.multiple_of(c * PAIR, PAIR), PAIR)
        term = jnp.dot(
            states[0, :, part], w_v[0, part, cols], preferred_element_type=F32
        )

        @pl.when(n == 0)
        def _():
            first[...] = term

        @pl.when(n > 0)
        def _():
            first[...] += term

        @pl.when(n == 1)
        def _():
            kv_send[c] = first[...].astype(BF16)

        @pl.when(i == 1)
        def _():
            pl.semaphore_wait(barrier, 8)

        @pl.when(n == 1)
        def _():
            kv_copy(c).start()

        @pl.when(i == 1)
        def _():
            cross_copy(0).start()
            cross_copy(1).start()

        return 0

    lax.fori_loop(0, 4, first_part, 0)

    def make(i, _):
        own_part = jnp.minimum(i // 2, 1)
        w = lax.rem(i, 3)

        @pl.when(i == 1)
        def _():
            load_x.start()
            load_q.start()
            load_kv1[0].wait()
            load_kv1[1].wait()

        @pl.when(i == 2)
        def _():
            load_x.wait()
            load_q.wait()
            load_wo.start()

        made[i] = jnp.dot(
            states[own_part], w_v[w], preferred_element_type=F32
        ).astype(BF16)

        @pl.when(i == 1)
        def _():
            for c in range(2):
                kv_send[2 + c] = made[1, :, c * PAIR : (c + 1) * PAIR]
                kv_copy(2 + c).start()

        @pl.when(i == 2)
        def _():
            cross_copy(0).wait_recv()
            z_copy(1, 0, z).start()
            z_copy(-1, 0, z).start()

        @pl.when(i == 4)
        def _():
            cross_copy(1).wait_recv()
            z_copy(1, 1, z).start()
            z_copy(-1, 1, z).start()
            sibling_copy(0, core).start()
            cross_copy(2).start()

        return 0

    def phase(ph, _):
        lax.fori_loop(1 + 3 * ph, 4 + ph, make, 0)
        kv_copy(2 * ph).wait_recv()
        kv_copy(2 * ph + 1).wait_recv()
        attend((ph,), 0)
        ctx_copy(ph).start()
        return 0

    load_lens.wait()
    lax.fori_loop(0, 2, phase, 0)
    cross_copy(3).start()
    attend((0, 1), 1)
    load_wo.wait()

    def both_pairs(ref, at_pair):
        return jnp.concatenate([ref[at_pair], ref[at_pair + 1]], axis=1)

    def local_step(i, _):
        cols = pl.ds(pl.multiple_of(i * 1024, 1024), 1024)
        p_loc[:, cols] = jnp.dot(
            both_pairs(ctx, 2), wo_v[:, cols], preferred_element_type=F32
        )
        return 0

    lax.fori_loop(0, 4, local_step, 0)
    ctx_copy(0).wait_recv()
    ctx_copy(1).wait_recv()

    def tile_of(k):
        j = k // 2
        off = j + j // 2 - 2 * (j // 3)
        par = lax.rem(k, 2)
        return tile(z + off, core + par * (1 - 2 * core))

    def far_copy(k):
        sgn = 1 - 2 * lax.rem(k, 2)
        return remote(
            p_buf.at[k, pl.ds(0, 64)], r1.at[k], r1s.at[k], r1r.at[k], along_x(sgn)
        )

    def back_copy(k):
        par = lax.rem(k, 2)
        rows = pl.ds(pl.multiple_of(128 - 64 * par, 64), 64)
        return remote(
            p_buf.at[k, rows], rb.at[k], rbs.at[k], rbr.at[k], along_x(2 * par - 1)
        )

    def fwd_rows(k):
        return pl.ds(pl.multiple_of(64 + 64 * lax.rem(k, 2), 64), 64)

    def fwd_copy(k):
        return remote(
            p_buf.at[k, fwd_rows(k)],
            rf.at[k],
            rfs.at[k],
            rfr.at[k],
            along_x(1 - 2 * lax.rem(k, 2)),
        )

    def project_tile(k):
        g = tile_of(k)
        cols = pl.ds(pl.multiple_of(g * TW, TW), TW)
        acc = p_loc[:, cols] + jnp.dot(
            both_pairs(ctx_recv, 0), wof[g], preferred_element_type=F32
        )
        p_buf[k] = acc.astype(BF16)
        far_copy(k).start()
        back_copy(k).start()

    def combine(k):
        far_copy(k).wait_recv()
        rows = fwd_rows(k)
        p_buf[k, rows] = (p_buf[k, rows].astype(F32) + r1[k].astype(F32)).astype(BF16)
        fwd_copy(k).start()

    def finish(k):
        back_copy(k).wait_recv()
        fwd_copy(k).wait_recv()
        g = tile_of(k)
        cols = pl.ds(pl.multiple_of(g * TW, TW), TW)
        out_ref[:, cols] = (
            p_buf[k, 192:256].astype(F32) + rb[k].astype(F32) + rf[k].astype(F32)
        ).astype(BF16)

    def out_step(k, _):
        @pl.when(k >= 3)
        def _():
            combine(k - 3)

        for j in range(4):

            @pl.when(k == 2 * j)
            def _(j=j):
                if j == 1:
                    z_copy(-1, 0, z + 1).wait_recv()
                    z_copy(-1, 1, z + 1).wait_recv()
                if j == 2:
                    z_copy(1, 0, z - 1).wait_recv()
                    z_copy(1, 1, z - 1).wait_recv()
                if j == 3:
                    cross_copy(2).wait_recv()
                    cross_copy(3).wait_recv()
                if j > 0:
                    sibling_copy(j, core).start()

            @pl.when(k == 2 * j + 1)
            def _(j=j):
                sibling_copy(j, 1 - core).wait_recv()

        @pl.when(k < NT)
        def _():
            project_tile(k)

        return 0

    lax.fori_loop(0, NT + 3, out_step, 0)

    def last_step(k, _):
        finish(k)
        return 0

    lax.fori_loop(0, NT, last_step, 0)

    for c in range(4):
        sibling_copy(c, core).wait_send()
        cross_copy(c).wait_send()
        kv_copy(c).wait_send()
    for pair in range(2):
        ctx_copy(pair).wait_send()
    for i in range(2):
        z_copy(1, i, z).wait_send()
        z_copy(-1, i, z).wait_send()

    def drain(k, _):
        far_copy(k).wait_send()
        back_copy(k).wait_send()
        fwd_copy(k).wait_send()
        return 0

    lax.fori_loop(0, NT, drain, 0)


def body(layer_input, memory, seg_lengths, query_weight, key_weight, value_weight, out_weight):
    dma = pltpu.SemaphoreType.DMA
    out = pl.pallas_call(
        kernel,
        out_shape=jax.ShapeDtypeStruct((64, D), BF16),
        in_specs=[pl.BlockSpec(memory_space=pltpu.HBM)] * 7,
        out_specs=pl.BlockSpec(memory_space=pltpu.VMEM),
        scratch_shapes=[
            pltpu.SMEM((16,), jnp.int32),
            pltpu.VMEM((2, SEG, D), BF16),
            pltpu.VMEM((3, D, COLS), BF16),
            pltpu.VMEM((COLS, D), BF16),
            pltpu.VMEM((NT, COLS, TW), BF16),
            pltpu.VMEM((4, SEG, PAIR), BF16),
            pltpu.VMEM((4, SEG, PAIR), BF16),
            pltpu.VMEM((5, SEG, COLS), BF16),
            pltpu.VMEM((4, 256, PAIR), BF16),
            pltpu.VMEM((2, 256, PAIR), BF16),
            pltpu.VMEM((SEG, PAIR), F32),
            pltpu.VMEM((256, D), F32),
            pltpu.VMEM((NT, 256, TW), BF16),
            pltpu.VMEM((NT, 64, TW), BF16),
            pltpu.VMEM((NT, 64, TW), BF16),
            pltpu.VMEM((NT, 64, TW), BF16),
            dma((18,)),
            dma((4,)),
            dma((4,)),
            dma((2,)),
            dma((2,)),
            dma((4,)),
            dma((4,)),
            dma((4,)),
            dma((4,)),
            dma((4,)),
            dma((4,)),
            dma((NT,)),
            dma((NT,)),
            dma((NT,)),
            dma((NT,)),
            dma((NT,)),
            dma((NT,)),
        ],
        compiler_params=pltpu.CompilerParams(
            collective_id=0, has_side_effects=True, vmem_limit_bytes=50 * 2**20
        ),
    )(
        seg_lengths,
        layer_input,
        memory,
        query_weight,
        key_weight,
        value_weight,
        out_weight,
    )
    return out[None]


def solution(mesh):
    return jax.shard_map(
        body,
        mesh=mesh,
        in_specs=(
            P("seq", None, None),
            P("seq", None, None),
            P(),
            P(None, "tp"),
            P(None, "tp"),
            P(None, "tp"),
            P("tp", None),
        ),
        out_specs=P("seq", "tp", None),
        check_vma=False,
    )
```
